128 devices in a mesh: grp: 4 (over x_lo, core), seq: 32 (over z, x_hi, y).
Axes of the slice: x: 4 (x_hi: 2, x_lo: 2; x = x_hi * 2 + x_lo), y: 4, z: 4, core: 2. Of those that a mesh axis runs over, the one named last changes fastest.
Arguments:
- branch_query: bfloat16 [128, 128, 4096], P(('grp', 'seq')), may hold values from -36 to 36
- branch_key: bfloat16 [128, 128, 512], P(('grp', 'seq')), may hold values from -36 to 36
- branch_value_rows: bfloat16 [128, 128, 512], P(('grp', 'seq')), may hold values from -6 to 6
- prefix_key_rows: bfloat16 [8192, 512], P(('grp', 'seq')), may hold values from -6 to 6
- prefix_value_rows: bfloat16 [8192, 512], P(('grp', 'seq')), may hold values from -6 to 6
- grad_out: bfloat16 [128, 128, 4096], P(('grp', 'seq')), may hold values from -6 to 6
- branch_length: int32 [128], P(('grp', 'seq')), may hold values from 64 to 128
- branch_prefix: int32 [128], P(('grp', 'seq')), may hold values from 0 to 3
- replay_count: int32 [128], P(('grp', 'seq')), may hold values from 1 to 16
Outputs:
- grad_query: bfloat16 [128, 128, 4096], P(('grp', 'seq'))
- grad_branch_key: bfloat16 [128, 128, 512], P(('grp', 'seq'))
- grad_branch_value: bfloat16 [128, 128, 512], P(('grp', 'seq'))
- grad_prefix_key: bfloat16 [8192, 512], P(('grp', 'seq'))
The draws below stay inside these ranges and needn't reach their ends.
All inputs are finite; a program needn't handle non-finite values.
Results may differ from the reference program's by a relative error of at most 0.013.
Values may be sent and summed in bfloat16 or wider, within the bound.
A program may use at most 128 MiB of HBM per device.

```python
import math
import jax
import jax.numpy as jnp
import numpy as np
from jax import lax

QUERY_HEADS = 32
SHARED_KV_LANES = 4
ATTN_DIMENSION = 128
BRANCH_SLOTS = 128
BRANCH_COUNT = 128
PREFIX_COUNT = 4
STEM_TOKENS = 2048


def draw_branch_key(key, part):
    key = jax.random.fold_in(key, 11)
    leading_key = jax.random.fold_in(key, 0)
    return jnp.clip(jax.random.normal(leading_key, (BRANCH_COUNT, BRANCH_SLOTS, SHARED_KV_LANES * ATTN_DIMENSION), jnp.float32), -6.0, 6.0).astype(jnp.bfloat16)


def draw_branch_query(key, part):
    key = jax.random.fold_in(key, 12)
    leading_key = jax.random.fold_in(key, 0)
    return jnp.clip(jax.random.normal(leading_key, (BRANCH_COUNT, BRANCH_SLOTS, QUERY_HEADS * ATTN_DIMENSION), jnp.float32), -6.0, 6.0).astype(jnp.bfloat16)


def place_ends(array, own_key, smallest, top_value):
    longest = array.shape.index(max(array.shape))
    spots = []
    for shift in (0, 1):
        where = [jax.random.randint(jax.random.fold_in(own_key, axis), (), 0, length) for axis, length in enumerate(array.shape)]
        where[longest] = (where[longest] + shift) % array.shape[longest]
        spots.append(tuple(where))
    return array.at[spots[0]].set(smallest).at[spots[1]].set(top_value)


def block_scale(key, shape, cuts, smallest, high):
    level = 1.0
    for position, blocks in cuts:
        heights = jax.random.uniform(jax.random.fold_in(jax.random.fold_in(key, 6), position), (blocks,), jnp.float32, smallest / len(cuts), high / len(cuts))
        level = level * jnp.repeat(jnp.exp(heights), shape[position] // blocks).reshape((-1,) + (1,) * (len(shape) - 1 - position))
    return level


def rank_bounds(number_of, lean):
    portions = [(1 << 20) // math.isqrt(rank ** lean) + 1 for rank in range(1, number_of + 1)]
    deviation = 1 + sum(portions) // (1 << 30)
    return np.cumsum(np.array([max(1, weight // deviation) for weight in portions]))


def skewed_ids(key, extent, count, skew):
    listing = rank_bounds(count, skew)
    lot = jax.random.randint(jax.random.fold_in(key, 1), extent, 0, int(listing[count - 1]))
    standing = jnp.searchsorted(jnp.asarray(listing, jnp.int32), lot, side="right")
    return jax.random.permutation(jax.random.fold_in(key, 2), count)[standing].astype(jnp.int32)


def normal_values(key, dims, scale, bound, cuts=(), kind=jnp.bfloat16):
    gain = block_scale(key, dims, cuts, -0.22, 0.18) if cuts else 1.0
    entries = jax.random.normal(key, dims, jnp.float32) * scale * gain
    return jnp.minimum(jnp.maximum(entries, -bound), bound).astype(kind)


def setup_inputs(seed: int = 0) -> dict:
    splits = jax.random.split(jax.random.key(seed), 10)
    return {
        "branch_query": draw_branch_query(jax.random.fold_in(splits[9], 71), 0),
        "branch_key": draw_branch_key(jax.random.fold_in(splits[9], 71), 0),
        "branch_value_rows": normal_values(splits[2], (BRANCH_COUNT, BRANCH_SLOTS, SHARED_KV_LANES * ATTN_DIMENSION), 1.0, 6.0, ((0, 128),)),
        "prefix_key_rows": normal_values(splits[3], (PREFIX_COUNT * STEM_TOKENS, SHARED_KV_LANES * ATTN_DIMENSION), 1.0, 6.0, ((0, 128),)),
        "prefix_value_rows": normal_values(splits[4], (PREFIX_COUNT * STEM_TOKENS, SHARED_KV_LANES * ATTN_DIMENSION), 1.0, 6.0, ((0, 128),)),
        "grad_out": normal_values(splits[5], (BRANCH_COUNT, BRANCH_SLOTS, QUERY_HEADS * ATTN_DIMENSION), 1.0, 6.0, ((0, 128),)),
        "branch_length": place_ends(jax.random.randint(splits[6], (BRANCH_COUNT,), BRANCH_SLOTS // 2, BRANCH_SLOTS + 1), jax.random.fold_in(splits[6], 1), BRANCH_SLOTS // 2, BRANCH_SLOTS).astype(jnp.int32),
        "branch_prefix": place_ends(skewed_ids(splits[7], (BRANCH_COUNT,), PREFIX_COUNT, 2), jax.random.fold_in(splits[7], 3), 0, PREFIX_COUNT - 1).astype(jnp.int32),
        "replay_count": place_ends(jax.random.randint(splits[8], (BRANCH_COUNT,), 1, 17), jax.random.fold_in(splits[8], 1), 1, 16).astype(jnp.int32),
    }


def twig_reverse_pass(asker_entries, key_matrix, value_matrix, adjoint_seed, sequence_extent, rerun_episodes):
    row_total = asker_entries.shape[0]
    lookup_aggregate = key_matrix.shape[0]
    prefix_span = lookup_aggregate - row_total
    group_width = QUERY_HEADS // SHARED_KV_LANES
    reciprocal_dimension_scale = 1.0 / math.sqrt(ATTN_DIMENSION)
    asker_array4 = asker_entries.astype(jnp.float32).reshape(row_total, SHARED_KV_LANES, group_width, ATTN_DIMENSION)
    key_tensor3 = key_matrix.astype(jnp.float32).reshape(lookup_aggregate, SHARED_KV_LANES, ATTN_DIMENSION)
    value_tensor3 = value_matrix.astype(jnp.float32).reshape(lookup_aggregate, SHARED_KV_LANES, ATTN_DIMENSION)
    scores = jnp.einsum('lgrd,sgd->grls', asker_array4, key_tensor3) * reciprocal_dimension_scale
    visible = jnp.arange(lookup_aggregate)[None, :] <= prefix_span + jnp.arange(row_total)[:, None]
    scores = jnp.where(visible, scores, jnp.float32(-1e+30))
    row_max = lax.optimization_barrier(jnp.max(scores, axis=-1, keepdims=True))
    exponent = jnp.exp(scores - row_max)
    probs = exponent / lax.optimization_barrier(jnp.sum(exponent, axis=-1, keepdims=True))
    softmax_lowered_precision = lax.optimization_barrier(probs.astype(jnp.bfloat16)).astype(jnp.float32)
    attended = jnp.einsum('grls,sgd->lgrd', softmax_lowered_precision, value_tensor3)
    weights = (jnp.arange(row_total) < sequence_extent).astype(jnp.float32) * lax.rsqrt(rerun_episodes.astype(jnp.float32))
    weighted_output = lax.optimization_barrier((adjoint_seed.astype(jnp.float32) * weights[:, None]).astype(jnp.bfloat16))
    mixed_result_array4 = weighted_output.astype(jnp.float32).reshape(row_total, SHARED_KV_LANES, group_width, ATTN_DIMENSION)
    row_delta = jnp.transpose(lax.optimization_barrier(jnp.sum(mixed_result_array4 * attended, axis=3)), (1, 2, 0))[..., None]
    dprobs = jnp.einsum('lgrd,sgd->grls', mixed_result_array4, value_tensor3)
    logit_derivative = lax.optimization_barrier((probs * (dprobs - row_delta)).astype(jnp.bfloat16)).astype(jnp.float32)
    derivative_of_asker = (jnp.einsum('grls,sgd->lgrd', logit_derivative, key_tensor3) * reciprocal_dimension_scale).reshape(row_total, QUERY_HEADS * ATTN_DIMENSION)
    lookup_contributions = (jnp.einsum('prno,nprg->opg', logit_derivative, asker_array4) * reciprocal_dimension_scale).reshape(lookup_aggregate, SHARED_KV_LANES * ATTN_DIMENSION)
    payload_contributions = jnp.einsum('prno,nprg->opg', softmax_lowered_precision, mixed_result_array4).reshape(lookup_aggregate, SHARED_KV_LANES * ATTN_DIMENSION)
    return (derivative_of_asker.astype(jnp.bfloat16), lookup_contributions, payload_contributions)

def reference(branch_query, branch_key, branch_value_rows, prefix_key_rows, prefix_value_rows, grad_out, branch_length, branch_prefix, replay_count):
    width_total = SHARED_KV_LANES * ATTN_DIMENSION
    prefix_keys = prefix_key_rows.reshape(PREFIX_COUNT, STEM_TOKENS, width_total)
    prefix_values = prefix_value_rows.reshape(PREFIX_COUNT, STEM_TOKENS, width_total)

    def one_branch(lookup_accumulated, pieces):
        asker_entries, key_matrix, value_matrix, adjoint_seed, sequence_extent, holder_position, rerun_episodes = pieces
        owner_keys = lax.dynamic_index_in_dim(prefix_keys, holder_position, 0, keepdims=False)
        owner_values = lax.dynamic_index_in_dim(prefix_values, holder_position, 0, keepdims=False)
        every_lookup_entry = jnp.concatenate([owner_keys, key_matrix], axis=0)
        every_payload_entry = jnp.concatenate([owner_values, value_matrix], axis=0)
        derivative_of_asker, lookup_contributions, payload_contributions = twig_reverse_pass(asker_entries, every_lookup_entry, every_payload_entry, adjoint_seed, sequence_extent, rerun_episodes)
        lookup_accumulated = lookup_accumulated.at[holder_position].add(lookup_contributions[:STEM_TOKENS])
        results_list = (derivative_of_asker, lookup_contributions[STEM_TOKENS:].astype(jnp.bfloat16), payload_contributions[STEM_TOKENS:].astype(jnp.bfloat16))
        return (lookup_accumulated, results_list)
    start_sums = jnp.zeros((PREFIX_COUNT, STEM_TOKENS, width_total), jnp.float32)
    sums, results_list = lax.scan(one_branch, start_sums, (branch_query, branch_key, branch_value_rows, grad_out, branch_length, branch_prefix, replay_count))
    grad_query, grad_branch_key, grad_branch_value = results_list
    grad_prefix_key = sums.reshape(PREFIX_COUNT * STEM_TOKENS, width_total).astype(jnp.bfloat16)
    return (grad_query, grad_branch_key, grad_branch_value, grad_prefix_key)
```

```python
import functools
import math

import jax
import jax.numpy as jnp
from jax import lax
from jax.experimental import pallas as pl
from jax.experimental.pallas import tpu as pltpu
from jax.sharding import PartitionSpec as P

f32, bf16 = jnp.float32, jnp.bfloat16
MESH = pl.DeviceIdType.MESH
SCALE = 1.0 / math.sqrt(128.0)
EXP2_SCALE = math.log2(math.e) / math.sqrt(128.0)
NEG = -1e30
HALVES = (("y", "z"), ("z", "y"))
HEADS, BRANCHES, KV = 2, 2, 2


def dot(a, b, ca, cb):
    return lax.dot_general(a, b, (((ca,), (cb,)), ((), ())), preferred_element_type=f32)


def place():
    g, s = lax.axis_index("grp"), lax.axis_index("seq")
    return dict(x=((s // 4) % 2) * 2 + g // 2, y=s % 4, z=s // 8, core=g % 2)


def device(at):
    return ((at["x"] % 2) * 2 + at["core"], at["z"] * 8 + (at["x"] // 2) * 4 + at["y"])


def peer(at, axis, distance, other_core=0):
    to = dict(at)
    if axis is not None:
        to[axis] = (at[axis] + distance) % 4
    if other_core:
        to["core"] = 1 - at["core"]
    return device(to)


def kernel(
    q_hbm, bk_ref, bv_ref, pk_ref, pv_ref, go_hbm, len_ref, pfx_ref, cnt_ref,
    dq_hbm, dbk_hbm, dbv_hbm, dpk_ref,
    go_s, qb, wb, w_send, kbr, vbr, id_own, id_in, id_s,
    pack, g1, pick, ksel, s_s, p_s, ds_s, dk_s, dv_s, dq_s, dbk_s, dbv_s,
    dkb, r1, s2, r2, s3, r3,
    send_sem, recv_sem, local_sem,
):
    at = place()
    core = at["core"]
    other = 1 - core
    counter = [0]
    started = []

    def send(src, dst, to):
        k = counter[0]
        counter[0] += 1
        copy = pltpu.make_async_remote_copy(
            src_ref=src, dst_ref=dst, send_sem=send_sem.at[k], recv_sem=recv_sem.at[k],
            device_id=to, device_id_type=MESH,
        )
        copy.start()
        started.append(copy)
        return copy

    def cols(start, size):
        return pl.ds(pl.multiple_of(start, 128), size)

    go_copy = pltpu.make_async_copy(go_hbm, go_s, local_sem.at[0])
    q_copy = pltpu.make_async_copy(q_hbm.at[:, cols(core * 2048, 2048)], qb.at[0], local_sem.at[1])
    go_copy.start()
    q_copy.start()
    for half in range(2):
        for head in range(4):
            rows, c128 = slice(half * 32, half * 32 + 32), slice(head * 128, head * 128 + 128)
            pack[half, head, 0] = pk_ref[rows, c128]
            pack[half, head, 1] = pv_ref[rows, c128]
    id_tile = jnp.full((8, 128), pfx_ref[0], jnp.int32)
    id_own[...] = id_tile
    id_in[core] = id_tile

    barrier = pltpu.get_barrier_semaphore()
    partners = [peer(at, None, 0, 1)] + [peer(at, "x", d) for d in (1, 2, 3)]
    partners += [peer(at, a, d, o) for a in "yz" for d in (1, 2, 3) for o in (0, 1)]
    for to in partners:
        pl.semaphore_signal(barrier, inc=1, device_id=to, device_id_type=MESH)
    pl.semaphore_wait(barrier, len(partners))

    def id_slot(half, d, c):
        return c if d == 0 else 2 + half * 6 + (d - 1) * 2 + c

    id_copies = [send(id_own, id_in.at[core], peer(at, None, 0, 1))]
    for half, (_, last) in enumerate(HALVES):
        for d in (1, 2, 3):
            for o in (0, 1):
                id_copies.append(send(id_own, id_in.at[id_slot(half, d, core)], peer(at, last, 4 - d, o)))

    first_copies = []
    for half, (first, _) in enumerate(HALVES):
        here = (slice(None), slice(None), at["x"], at[first], core)
        for d in range(4):
            for o in (0, 1):
                if d == 0 and o == 0:
                    continue
                to_core = other if o else core
                first_copies.append(
                    send(
                        pack.at[half, pl.ds(2 * to_core, 2)],
                        g1.at[(half,) + here],
                        peer(at, first if d else None, d, o),
                    )
                )
        g1[(half,) + here] = pack[half, pl.ds(2 * core, 2)]

    pair = peer(at, None, 0, 1)
    pair_copies = [
        send(q_hbm.at[:, cols(other * 2048, 2048)], qb.at[1], pair),
        send(bk_ref.at[:, cols(other * 256, 256)], kbr.at[1], pair),
        send(bv_ref.at[:, cols(other * 256, 256)], vbr.at[1], pair),
    ]
    kbr[0] = bk_ref[:, cols(core * 256, 256)]
    vbr[0] = bv_ref[:, cols(core * 256, 256)]
    go_copy.wait()
    weight = lax.rsqrt(jnp.full((128, 128), cnt_ref[0], jnp.int32).astype(f32))
    live = lax.broadcasted_iota(jnp.int32, (128, 128), 0) < len_ref[0]
    weight = jnp.where(live, weight, 0.0)

    def weigh(i, _):
        theirs = go_s[:, cols(other * 2048 + i * 128, 128)].astype(f32) * weight
        w_send[:, cols(i * 128, 128)] = theirs.astype(bf16)
        ours = go_s[:, cols(core * 2048 + i * 128, 128)].astype(f32) * weight
        wb[0, :, cols(i * 128, 128)] = ours.astype(bf16)
        return 0

    lax.fori_loop(0, 16, weigh, 0)
    pair_copies.append(send(w_send, wb.at[1], pair))

    for copy in first_copies:
        copy.wait_recv()
    second_copies = {}
    for h in range(HEADS):
        for kv in range(KV):
            for half in range(2):
                block = g1.at[half, h, kv, at["x"]]
                second_copies[h, kv, half] = [send(block, block, peer(at, "x", d)) for d in (1, 2, 3)]

    for copy in id_copies:
        copy.wait_recv()
    id_copy = pltpu.make_async_copy(id_in, id_s, local_sem.at[2])
    id_copy.start()
    id_copy.wait()

    def prefix_of(half, d, b):
        return id_s[id_slot(half, d, other if b else core), 0, 0]

    last_copies = {h: [] for h in range(HEADS)}
    for h in range(HEADS):
        for kv in range(KV):
            for half, (_, last) in enumerate(HALVES):
                for copy in second_copies[h, kv, half]:
                    copy.wait_recv()
                for d in (1, 2, 3, 0):
                    for b in range(BRANCHES):
                        p = prefix_of(half, d, b)
                        for xh in range(2):
                            of = [g1[half, h, kv, xh * 2 + k // 2, :, k % 2].reshape(128, 128) for k in range(4)]
                            low = jnp.where(p == 0, of[0], of[1])
                            rows = jnp.where(p < 2, low, jnp.where(p == 2, of[2], of[3]))
                            if d:
                                pick[half, h, kv, d - 1, b, xh * 128:xh * 128 + 128] = rows
                            else:
                                ksel[h, kv, b, half, at[last], xh * 128:xh * 128 + 128] = rows
                    if d:
                        last_copies[h].append(
                            send(
                                pick.at[half, h, kv, d - 1],
                                ksel.at[h, kv, :, half, at[last]],
                                peer(at, last, d),
                            )
                        )

    q_copy.wait()
    for copy in pair_copies:
        copy.wait_recv()

    row = lax.broadcasted_iota(jnp.int32, (256, 128), 0) % 128
    seen = lax.broadcasted_iota(jnp.int32, (256, 128), 1) <= row

    def unit(h, b):
        local = slice(h * 128, h * 128 + 128)

        def keys(kv, i):
            if i == 8:
                return (kbr, vbr)[kv][b, :, local]
            return ksel[h, kv, b, i // 4, i % 4]

        spans = [(i, i * 256, 256) for i in range(8)] + [(8, 2048, 128)]

        def step(j, _):
            at0 = cols(h * 1024 + j * 256, 128)
            at1 = cols(h * 1024 + j * 256 + 128, 128)
            query = jnp.concatenate([qb[b, :, at0], qb[b, :, at1]], 0)
            weighted = jnp.concatenate([wb[b, :, at0], wb[b, :, at1]], 0)
            top = None
            for i, o, n in spans:
                s = dot(query, keys(0, i), 1, 1)
                if i == 8:
                    s = jnp.where(seen, s, NEG)
                s_s[:, o:o + n] = s
                for u in range(0, n, 128):
                    top = s[:, u:u + 128] if top is None else jnp.maximum(top, s[:, u:u + 128])
                p_s[:, o:o + n] = dot(weighted, keys(1, i), 1, 1)
            top = jnp.max(top, axis=1, keepdims=True) * EXP2_SCALE
            total = jnp.zeros((256, 128), f32)
            mixed = jnp.zeros((256, 128), f32)
            for i, o, n in spans:
                e = jnp.exp2(s_s[:, o:o + n] * EXP2_SCALE - top)
                s_s[:, o:o + n] = e
                ed = e * p_s[:, o:o + n]
                for u in range(0, n, 128):
                    total = total + e[:, u:u + 128]
                    mixed = mixed + ed[:, u:u + 128]
            inverse = 1.0 / jnp.sum(total, axis=1, keepdims=True)
            delta = jnp.sum(mixed, axis=1, keepdims=True) * inverse
            dq = None
            for i, o, n in spans:
                ds = (s_s[:, o:o + n] * (p_s[:, o:o + n] - delta)).astype(bf16)
                ds_s[:, o:o + n] = ds
                term = dot(ds, keys(0, i), 1, 0)
                dq = term if dq is None else dq + term
            dq = (dq * (inverse * SCALE)).astype(bf16)
            dq_s[b, :, at0] = dq[:128]
            dq_s[b, :, at1] = dq[128:]
            scaled = (query.astype(f32) * (inverse * SCALE)).astype(bf16)
            probs = (s_s[:, 2048:] * inverse).astype(bf16)
            dk = dot(ds_s[...], scaled, 0, 0)
            dv = dot(probs, weighted, 0, 0)

            @pl.when(j == 0)
            def _():
                dk_s[...] = dk
                dv_s[...] = dv

            @pl.when(j > 0)
            def _():
                dk_s[...] += dk
                dv_s[...] += dv

            return 0

        lax.fori_loop(0, 4, step, 0)
        dbk_s[b, :, local] = dk_s[2048:].astype(bf16)
        dbv_s[b, :, local] = dv_s[...].astype(bf16)
        for i in range(8):
            dkb[h, b, i // 4, i % 4] = dk_s[i * 256:i * 256 + 256].astype(bf16)

    def sum_last_send(h, b):
        copies = []
        for half, (_, last) in enumerate(HALVES):
            for d in (1, 2, 3):
                copies.append(
                    send(
                        dkb.at[h, b, half, (at[last] + d) % 4],
                        r1.at[h, half, d - 1, b],
                        peer(at, last, d),
                    )
                )
        return copies

    def sum_last(h, copies):
        for copy in copies:
            copy.wait_recv()
        for half, (_, last) in enumerate(HALVES):
            ids = {(d, b): prefix_of(half, (4 - d) % 4, b) for d in range(4) for b in range(BRANCHES)}

            def block(i, _):
                rows = pl.ds(pl.multiple_of(i * 32, 32), 32)
                sums = [jnp.zeros((32, 128), f32) for _ in range(4)]
                for d in range(4):
                    for b in range(BRANCHES):
                        if d:
                            term = r1[h, half, d - 1, b, rows, :]
                        else:
                            term = dkb[h, b, half, at[last], rows, :]
                        term = term.astype(f32)
                        for p in range(4):
                            sums[p] = sums[p] + jnp.where(ids[d, b] == p, term, 0.0)
                for p in range(4):
                    s2[h, half, (i // 4) * 2 + p // 2, i % 4, p % 2] = sums[p].astype(bf16)
                return 0

            lax.fori_loop(0, 8, block, 0)

    def sum_x_send(h):
        return [
            send(s2.at[h, half, (at["x"] + d) % 4], r2.at[h, half, d - 1], peer(at, "x", d))
            for half in range(2)
            for d in (1, 2, 3)
        ]

    def sum_x(h, copies):
        for copy in copies:
            copy.wait_recv()
        for half in range(2):
            for f in range(4):
                total = s2[h, half, at["x"], f].astype(f32)
                for d in range(3):
                    total = total + r2[h, half, d, f].astype(f32)
                s3[h, half, f] = total.astype(bf16)

    def sum_first_send(h):
        copies = []
        for half, (first, _) in enumerate(HALVES):
            for d in range(4):
                for o in (0, 1):
                    if d == 0 and o == 0:
                        continue
                    to_core = other if o else core
                    copies.append(
                        send(
                            s3.at[h, half, (at[first] + d) % 4, to_core],
                            r3.at[h, half, d, o],
                            peer(at, first if d else None, d, o),
                        )
                    )
        return copies

    def sum_first(h, copies):
        for copy in copies:
            copy.wait_recv()
        for half, (first, _) in enumerate(HALVES):
            for o in (0, 1):
                total = (r3[h, half, 0, 1] if o else s3[h, half, at[first], core]).astype(f32)
                for d in (1, 2, 3):
                    total = total + r3[h, half, d, o].astype(f32)
                head = 2 * (other if o else core) + h
                dpk_ref[half * 32:half * 32 + 32, cols(head * 128, 128)] = total.astype(bf16)

    local_copies = []

    def give_back(h, b, n):
        heads = cols(core * 2048 + h * 1024, 1024)
        src, dst = dq_s.at[b, :, h * 1024:h * 1024 + 1024], dq_hbm.at[:, heads]
        if b:
            return [send(src, dst, pair)]
        copy = pltpu.make_async_copy(src, dst, local_sem.at[n])
        copy.start()
        local_copies.append(copy)
        return []

    returned = []
    for copy in last_copies[0]:
        copy.wait_recv()
    unit(0, 1)
    last0 = sum_last_send(0, 1)
    returned += give_back(0, 1, 3)
    unit(0, 0)
    last0 += sum_last_send(0, 0)
    returned += give_back(0, 0, 3)
    for copy in last_copies[1]:
        copy.wait_recv()
    unit(1, 1)
    last1 = sum_last_send(1, 1)
    returned += give_back(1, 1, 4)
    mine = cols(core * 256, 256)
    returned.append(send(dbk_s.at[1], dbk_hbm.at[:, mine], pair))
    returned.append(send(dbv_s.at[1], dbv_hbm.at[:, mine], pair))
    sum_last(0, last0)
    x0 = sum_x_send(0)
    unit(1, 0)
    last1 += sum_last_send(1, 0)
    returned += give_back(1, 0, 4)
    for n, (src, dst) in enumerate(((dbk_s, dbk_hbm), (dbv_s, dbv_hbm))):
        copy = pltpu.make_async_copy(src.at[0], dst.at[:, mine], local_sem.at[5 + n])
        copy.start()
        local_copies.append(copy)
    sum_x(0, x0)
    first0 = sum_first_send(0)
    sum_last(1, last1)
    x1 = sum_x_send(1)
    sum_first(0, first0)
    sum_x(1, x1)
    first1 = sum_first_send(1)
    sum_first(1, first1)

    for copy in returned:
        copy.wait_recv()
    for copy in local_copies:
        copy.wait()
    for copy in started:
        copy.wait_send()


COPIES = 13 + 14 + 4 + 24 + 24 + 24 + 12 + 28 + 4
ANY = pl.BlockSpec(memory_space=pl.ANY)
VMEM = pl.BlockSpec(memory_space=pltpu.VMEM)
SMEM = pl.BlockSpec(memory_space=pltpu.SMEM)


def on_device(bq, bk, bv, pk, pv, go, length, prefix, count):
    v = pltpu.VMEM
    outs = pl.pallas_call(
        kernel,
        out_shape=(
            jax.ShapeDtypeStruct((128, 4096), bf16),
            jax.ShapeDtypeStruct((128, 512), bf16),
            jax.ShapeDtypeStruct((128, 512), bf16),
            jax.ShapeDtypeStruct((64, 512), bf16),
        ),
        in_specs=[ANY, VMEM, VMEM, VMEM, VMEM, ANY, SMEM, SMEM, SMEM],
        out_specs=(ANY, ANY, ANY, VMEM),
        scratch_shapes=[
            v((128, 4096), bf16),
            v((2, 128, 2048), bf16),
            v((2, 128, 2048), bf16),
            v((128, 2048), bf16),
            v((2, 128, 256), bf16),
            v((2, 128, 256), bf16),
            v((8, 128), jnp.int32),
            v((14, 8, 128), jnp.int32),
            pltpu.SMEM((14, 8, 128), jnp.int32),
            v((2, 4, 2, 32, 128), bf16),
            v((2, 2, 2, 4, 4, 2, 32, 128), bf16),
            v((2, 2, 2, 3, 2, 256, 128), bf16),
            v((2, 2, 2, 2, 4, 256, 128), bf16),
            v((256, 2176), f32),
            v((256, 2176), f32),
            v((256, 2176), bf16),
            v((2176, 128), f32),
            v((128, 128), f32),
            v((2, 128, 2048), bf16),
            v((2, 128, 256), bf16),
            v((2, 128, 256), bf16),
            v((2, 2, 2, 4, 256, 128), bf16),
            v((2, 2, 3, 2, 256, 128), bf16),
            v((2, 2, 4, 4, 2, 32, 128), bf16),
            v((2, 2, 3, 4, 2, 32, 128), bf16),
            v((2, 2, 4, 2, 32, 128), bf16),
            v((2, 2, 4, 2, 32, 128), bf16),
            pltpu.SemaphoreType.DMA((COPIES,)),
            pltpu.SemaphoreType.DMA((COPIES,)),
            pltpu.SemaphoreType.DMA((7,)),
        ],
        compiler_params=pltpu.CompilerParams(
            collective_id=0, has_side_effects=True, vmem_limit_bytes=56 * 1024 * 1024
        ),
        cost_estimate=pl.CostEstimate(flops=10**10, bytes_accessed=10**7, transcendentals=10**7),
    )(bq[0], bk[0], bv[0], pk, pv, go[0], length, prefix, count)
    return outs[0][None], outs[1][None], outs[2][None], outs[3]


def solution(mesh):
    both = ("grp", "seq")
    rows3, rows2, rows1 = P(both, None, None), P(both, None), P(both)
    return jax.shard_map(
        on_device,
        mesh=mesh,
        in_specs=(rows3, rows3, rows3, rows2, rows2, rows3, rows1, rows1, rows1),
        out_specs=(rows3, rows3, rows3, rows2),
        check_vma=False,
    )
```

```python
import functools
import math

import jax
import jax.numpy as jnp
from jax import lax
from jax.experimental import pallas as pl
from jax.experimental.pallas import tpu as pltpu
from jax.sharding import PartitionSpec as P

f32, bf16 = jnp.float32, jnp.bfloat16
MESH = pl.DeviceIdType.MESH
SCALE = 1.0 / math.sqrt(128.0)
EXP2_SCALE = math.log2(math.e) / math.sqrt(128.0)
NEG = -1e30
HALVES = (("y", "z"), ("z", "y"))
HEADS, BRANCHES, KV = 2, 2, 2


def dot(a, b, ca, cb):
    return lax.dot_general(a, b, (((ca,), (cb,)), ((), ())), preferred_element_type=f32)


def place():
    g, s = lax.axis_index("grp"), lax.axis_index("seq")
    return dict(x=((s // 4) % 2) * 2 + g // 2, y=s % 4, z=s // 8, core=g % 2)


def device(at):
    return ((at["x"] % 2) * 2 + at["core"], at["z"] * 8 + (at["x"] // 2) * 4 + at["y"])


def peer(at, axis, distance, other_core=0):
    to = dict(at)
    if axis is not None:
        to[axis] = (at[axis] + distance) % 4
    if other_core:
        to["core"] = 1 - at["core"]
    return device(to)


def kernel(
    q_hbm, bk_ref, bv_ref, pk_ref, pv_ref, go_hbm, len_ref, pfx_ref, cnt_ref,
    dq_hbm, dbk_hbm, dbv_hbm, dpk_ref,
    go_s, qb, wb, w_send, kbr, vbr, id_own, id_in, id_s,
    pack, g1, pick, ksel, s_s, p_s, ds_s, top_s, inv_s, pb_s, dk_s, dv_s, dq_s, dbk_s, dbv_s,
    dkb, r1, s2, r2, s3, r3,
    send_sem, recv_sem, local_sem,
):
    at = place()
    core = at["core"]
    other = 1 - core
    counter = [0]
    started = []

    def send(src, dst, to):
        k = counter[0]
        counter[0] += 1
        copy = pltpu.make_async_remote_copy(
            src_ref=src, dst_ref=dst, send_sem=send_sem.at[k], recv_sem=recv_sem.at[k],
            device_id=to, device_id_type=MESH,
        )
        copy.start()
        started.append(copy)
        return copy

    def cols(start, size):
        return pl.ds(pl.multiple_of(start, 128), size)

    go_copy = pltpu.make_async_copy(go_hbm, go_s, local_sem.at[0])
    q_copy = pltpu.make_async_copy(q_hbm.at[:, cols(core * 2048, 2048)], qb.at[0], local_sem.at[1])
    go_copy.start()
    q_copy.start()
    for half in range(2):
        for head in range(4):
            rows, c128 = slice(half * 32, half * 32 + 32), slice(head * 128, head * 128 + 128)
            pack[half, head, 0] = pk_ref[rows, c128]
            pack[half, head, 1] = pv_ref[rows, c128]
    id_tile = jnp.full((8, 128), pfx_ref[0], jnp.int32)
    id_own[...] = id_tile
    id_in[core] = id_tile

    barrier = pltpu.get_barrier_semaphore()
    partners = [peer(at, None, 0, 1)]
    partners += [peer(at, a, d, o) for a in "xyz" for d in (1, 2, 3) for o in (0, 1)]
    for to in partners:
        pl.semaphore_signal(barrier, inc=1, device_id=to, device_id_type=MESH)
    pl.semaphore_wait(barrier, len(partners))

    def grid(h, first):
        return (at[first], at["x"]) if h == 0 else (at["x"], at[first])

    first_copies = {}
    for h in range(HEADS):
        for half, (first, _) in enumerate(HALVES):
            here = (half, h, slice(None)) + grid(h, first) + (core,)
            first_copies[h, half] = []
            for d in range(4):
                for o in (0, 1):
                    if d == 0 and o == 0:
                        continue
                    to_core = other if o else core
                    axis = ("x" if h == 0 else first) if d else None
                    first_copies[h, half].append(
                        send(pack.at[half, 2 * to_core + h], g1.at[here], peer(at, axis, d, o))
                    )
            g1[here] = pack[half, 2 * core + h]

    def id_slot(half, d, c):
        return c if d == 0 else 2 + half * 6 + (d - 1) * 2 + c

    id_copies = [send(id_own, id_in.at[core], peer(at, None, 0, 1))]
    for half, (_, last) in enumerate(HALVES):
        for d in (1, 2, 3):
            for o in (0, 1):
                id_copies.append(send(id_own, id_in.at[id_slot(half, d, core)], peer(at, last, 4 - d, o)))

    pair = peer(at, None, 0, 1)
    pair_copies = [
        send(q_hbm.at[:, cols(other * 2048, 2048)], qb.at[1], pair),
        send(bk_ref.at[:, cols(other * 256, 256)], kbr.at[1], pair),
        send(bv_ref.at[:, cols(other * 256, 256)], vbr.at[1], pair),
    ]
    kbr[0] = bk_ref[:, cols(core * 256, 256)]
    vbr[0] = bv_ref[:, cols(core * 256, 256)]
    go_copy.wait()
    weight = lax.rsqrt(jnp.full((128, 128), cnt_ref[0], jnp.int32).astype(f32))
    live = lax.broadcasted_iota(jnp.int32, (128, 128), 0) < len_ref[0]
    weight = jnp.where(live, weight, 0.0)

    def weigh(i, _):
        theirs = go_s[:, cols(other * 2048 + i * 128, 128)].astype(f32) * weight
        w_send[:, cols(i * 128, 128)] = theirs.astype(bf16)
        ours = go_s[:, cols(core * 2048 + i * 128, 128)].astype(f32) * weight
        wb[0, :, cols(i * 128, 128)] = ours.astype(bf16)
        return 0

    lax.fori_loop(0, 16, weigh, 0)
    pair_copies.append(send(w_send, wb.at[1], pair))

    second_copies = {}
    for h in range(HEADS):
        for half in range(2):
            for copy in first_copies[h, half]:
                copy.wait_recv()
        for kv in range(KV):
            for half, (first, _) in enumerate(HALVES):
                axis = first if h == 0 else "x"
                block = g1.at[half, h, kv, at[axis]]
                second_copies[h, kv, half] = [send(block, block, peer(at, axis, d)) for d in (1, 2, 3)]

    for copy in id_copies:
        copy.wait_recv()
    id_copy = pltpu.make_async_copy(id_in, id_s, local_sem.at[2])
    id_copy.start()
    id_copy.wait()

    def prefix_of(half, d, b):
        return id_s[id_slot(half, d, other if b else core), 0, 0]

    last_copies = {(h, b): [] for h in range(HEADS) for b in range(BRANCHES)}

    def last_step(h, kv, half, b):
        last = HALVES[half][1]
        for d in (1, 2, 3, 0):
            p = prefix_of(half, d, b)
            for xh in range(2):
                of = []
                for k in range(4):
                    x = xh * 2 + k // 2
                    rows = g1[half, h, kv, :, x, k % 2] if h == 0 else g1[half, h, kv, x, :, k % 2]
                    of.append(rows.reshape(128, 128))
                low = jnp.where(p == 0, of[0], of[1])
                rows = jnp.where(p < 2, low, jnp.where(p == 2, of[2], of[3]))
                if d:
                    pick[half, h, kv, d - 1, b, xh * 128:xh * 128 + 128] = rows
                else:
                    ksel[h, kv, b, half, at[last], xh * 128:xh * 128 + 128] = rows
            if d:
                last_copies[h, b].append(
                    send(
                        pick.at[half, h, kv, d - 1, b],
                        ksel.at[h, kv, b, half, at[last]],
                        peer(at, last, d),
                    )
                )

    for h in range(HEADS):
        for b in (1, 0):
            for kv in range(KV):
                for half in range(2):
                    if b == 1:
                        for copy in second_copies[h, kv, half]:
                            copy.wait_recv()
                    last_step(h, kv, half, b)

    q_copy.wait()
    for copy in pair_copies:
        copy.wait_recv()

    spans = [(i, i * 256, 256) for i in range(8)] + [(8, 2048, 128)]

    def keys(kv, h, b, i):
        if i == 8:
            return (kbr, vbr)[kv][b, :, h * 128:h * 128 + 128]
        return ksel[h, kv, b, i // 4, i % 4]

    def rows_of(ref, t):
        h, b, j = t
        c = h * 1024 + j * 256
        return jnp.concatenate([ref[b, :, c:c + 128], ref[b, :, c + 128:c + 256]], 0)

    def split_query(t):
        query = rows_of(qb, t).astype(f32) * EXP2_SCALE
        high = query.astype(bf16)
        return jnp.concatenate([high, (query - high.astype(f32)).astype(bf16)], 1)

    def scores(t, slot, i, o, n, query, weighted):
        h, b, _ = t
        k = keys(0, h, b, i)
        s = dot(query, jnp.concatenate([k, k], 1), 1, 1)
        if i == 8:
            row = lax.broadcasted_iota(jnp.int32, (256, 128), 0) % 128
            s = jnp.where(lax.broadcasted_iota(jnp.int32, (256, 128), 1) <= row, s, NEG)
        s_s[slot, :, o:o + n] = s
        top = s[:, :128] if n == 128 else jnp.maximum(s[:, :128], s[:, 128:])
        top_s[slot] = top if i == 0 else jnp.maximum(top_s[slot], top)
        p_s[slot, :, o:o + n] = dot(weighted, keys(1, h, b, i), 1, 1)

    def softmax(slot, g):
        rows = slice(g * 32, g * 32 + 32)
        top = jnp.broadcast_to(jnp.max(top_s[slot, rows], axis=1, keepdims=True), (32, 128))
        total = mixed = None
        for o in range(0, 2176, 128):
            e = jnp.exp2(s_s[slot, rows, o:o + 128] - top)
            s_s[slot, rows, o:o + 128] = e
            ed = e * p_s[slot, rows, o:o + 128]
            total = e if total is None else total + e
            mixed = ed if mixed is None else mixed + ed
        inverse = 1.0 / jnp.sum(total, axis=1, keepdims=True)
        delta = jnp.broadcast_to(jnp.sum(mixed, axis=1, keepdims=True) * inverse, (32, 128))
        inv_s[slot, rows] = jnp.broadcast_to(inverse, (32, 128))
        for o in range(0, 2176, 128):
            e = s_s[slot, rows, o:o + 128]
            ds_s[slot, rows, o:o + 128] = (e * (p_s[slot, rows, o:o + 128] - delta)).astype(bf16)
            if o == 2048:
                pb_s[slot, rows] = (e * inverse).astype(bf16)

    def grad_query(t, slot):
        h, b, j = t
        scale = inv_s[slot] * SCALE
        dq = dot(ds_s[slot, :, :2048], ksel[h, 0, b].reshape(2048, 128), 1, 0)
        dq = dq + dot(ds_s[slot, :, 2048:], keys(0, h, b, 8), 1, 0)
        dq = (dq * scale).astype(bf16)
        c = h * 1024 + j * 256
        dq_s[b, :, c:c + 128] = dq[:128]
        dq_s[b, :, c + 128:c + 256] = dq[128:]
        dv = dot(pb_s[slot], rows_of(wb, t), 0, 0)
        dv_s[...] = dv if j == 0 else dv_s[...] + dv
        return (rows_of(qb, t).astype(f32) * scale).astype(bf16)

    def key_terms(t, slot, o, n, query):
        dk = dot(query, ds_s[slot, :, o:o + n], 0, 0)
        dk_s[:, o:o + n] = dk if t[2] == 0 else dk_s[:, o:o + n] + dk

    def finish_unit(h, b):
        local = slice(h * 128, h * 128 + 128)
        dbk_s[b, :, local] = dk_s[:, 2048:].T.astype(bf16)
        dbv_s[b, :, local] = dv_s[...].astype(bf16)
        for i in range(16):
            rows = slice(i % 2 * 128, i % 2 * 128 + 128)
            dkb[h, b, i // 8, i // 2 % 4, rows] = dk_s[:, i * 128:i * 128 + 128].T.astype(bf16)

    steps = [(h, b, j) for h in range(HEADS) for b in (1, 0) for j in range(4)]

    def pipeline(now):
        slot, before = now % 2, (now + 1) % 2
        ahead = steps[now] if now < 16 else None
        middle = steps[now - 1] if 0 < now <= 16 else None
        behind = steps[now - 2] if now >= 2 else None
        if ahead:
            query, weighted = split_query(ahead), rows_of(wb, ahead)
        if behind:
            scaled = grad_query(behind, slot)
        for i, o, n in spans:
            if ahead:
                scores(ahead, slot, i, o, n, query, weighted)
            if middle and i < 8:
                softmax(before, i)
            if behind:
                key_terms(behind, slot, o, n, scaled)
        if behind and behind[2] == 3:
            finish_unit(behind[0], behind[1])

    def sum_last_send(h, b):
        copies = []
        for half, (_, last) in enumerate(HALVES):
            for d in (1, 2, 3):
                copies.append(
                    send(
                        dkb.at[h, b, half, (at[last] + d) % 4],
                        r1.at[h, half, d - 1, b],
                        peer(at, last, d),
                    )
                )
        return copies

    def sum_last(h, copies):
        for copy in copies:
            copy.wait_recv()
        for half, (_, last) in enumerate(HALVES):
            ids = {(d, b): prefix_of(half, (4 - d) % 4, b) for d in range(4) for b in range(BRANCHES)}

            def block(i, _):
                rows = pl.ds(pl.multiple_of(i * 32, 32), 32)
                sums = [jnp.zeros((32, 128), f32) for _ in range(4)]
                for d in range(4):
                    for b in range(BRANCHES):
                        if d:
                            term = r1[h, half, d - 1, b, rows, :]
                        else:
                            term = dkb[h, b, half, at[last], rows, :]
                        term = term.astype(f32)
                        for p in range(4):
                            sums[p] = sums[p] + jnp.where(ids[d, b] == p, term, 0.0)
                for p in range(4):
                    s2[h, half, i % 4, (i // 4) * 2 + p // 2, p % 2] = sums[p].astype(bf16)
                return 0

            lax.fori_loop(0, 8, block, 0)

    def sum_first_send(h):
        return [
            send(s2.at[h, half, (at[first] + d) % 4], r2.at[h, half, d - 1], peer(at, first, d))
            for half, (first, _) in enumerate(HALVES)
            for d in (1, 2, 3)
        ]

    def sum_first(h, copies):
        for copy in copies:
            copy.wait_recv()
        for half, (first, _) in enumerate(HALVES):
            for x in range(4):
                total = s2[h, half, at[first], x].astype(f32)
                for d in range(3):
                    total = total + r2[h, half, d, x].astype(f32)
                s3[h, half, x] = total.astype(bf16)

    def sum_x_send(h):
        copies = []
        for half in range(2):
            for d in range(4):
                for o in (0, 1):
                    if d == 0 and o == 0:
                        continue
                    to_core = other if o else core
                    copies.append(
                        send(
                            s3.at[h, half, (at["x"] + d) % 4, to_core],
                            r3.at[h, half, d, o],
                            peer(at, "x" if d else None, d, o),
                        )
                    )
        return copies

    def sum_x(h, copies):
        for copy in copies:
            copy.wait_recv()
        for half in range(2):
            for o in (0, 1):
                total = (r3[h, half, 0, 1] if o else s3[h, half, at["x"], core]).astype(f32)
                for d in (1, 2, 3):
                    total = total + r3[h, half, d, o].astype(f32)
                head = 2 * (other if o else core) + h
                dpk_ref[half * 32:half * 32 + 32, cols(head * 128, 128)] = total.astype(bf16)

    local_copies = []

    def give_back(h, b, n):
        heads = cols(core * 2048 + h * 1024, 1024)
        src, dst = dq_s.at[b, :, h * 1024:h * 1024 + 1024], dq_hbm.at[:, heads]
        if b:
            return [send(src, dst, pair)]
        copy = pltpu.make_async_copy(src, dst, local_sem.at[n])
        copy.start()
        local_copies.append(copy)
        return []

    returned = []
    last_sums = {0: [], 1: []}
    mine = cols(core * 256, 256)
    for now in range(18):
        if now < 16 and now % 4 == 0:
            for copy in last_copies[steps[now][:2]]:
                copy.wait_recv()
        pipeline(now)
        if now in (5, 9, 13, 17):
            h, b, _ = steps[now - 2]
            last_sums[h] += sum_last_send(h, b)
            returned += give_back(h, b, 3 + h)
        if now == 13:
            returned.append(send(dbk_s.at[1], dbk_hbm.at[:, mine], pair))
            returned.append(send(dbv_s.at[1], dbv_hbm.at[:, mine], pair))
        if now == 15:
            sum_last(0, last_sums[0])
            first0 = sum_first_send(0)
    for n, (src, dst) in enumerate(((dbk_s, dbk_hbm), (dbv_s, dbv_hbm))):
        copy = pltpu.make_async_copy(src.at[0], dst.at[:, mine], local_sem.at[5 + n])
        copy.start()
        local_copies.append(copy)
    sum_first(0, first0)
    x0 = sum_x_send(0)
    sum_last(1, last_sums[1])
    first1 = sum_first_send(1)
    sum_x(0, x0)
    sum_first(1, first1)
    x1 = sum_x_send(1)
    sum_x(1, x1)

    for copy in returned:
        copy.wait_recv()
    for copy in local_copies:
        copy.wait()
    for copy in started:
        copy.wait_send()


COPIES = 13 + 28 + 4 + 24 + 48 + 24 + 12 + 28 + 4
ANY = pl.BlockSpec(memory_space=pl.ANY)
VMEM = pl.BlockSpec(memory_space=pltpu.VMEM)
SMEM = pl.BlockSpec(memory_space=pltpu.SMEM)


def on_device(bq, bk, bv, pk, pv, go, length, prefix, count):
    v = pltpu.VMEM
    outs = pl.pallas_call(
        kernel,
        out_shape=(
            jax.ShapeDtypeStruct((128, 4096), bf16),
            jax.ShapeDtypeStruct((128, 512), bf16),
            jax.ShapeDtypeStruct((128, 512), bf16),
            jax.ShapeDtypeStruct((64, 512), bf16),
        ),
        in_specs=[ANY, VMEM, VMEM, VMEM, VMEM, ANY, SMEM, SMEM, SMEM],
        out_specs=(ANY, ANY, ANY, VMEM),
        scratch_shapes=[
            v((128, 4096), bf16),
            v((2, 128, 2048), bf16),
            v((2, 128, 2048), bf16),
            v((128, 2048), bf16),
            v((2, 128, 256), bf16),
            v((2, 128, 256), bf16),
            v((8, 128), jnp.int32),
            v((14, 8, 128), jnp.int32),
            pltpu.SMEM((14, 8, 128), jnp.int32),
            v((2, 4, 2, 32, 128), bf16),
            v((2, 2, 2, 4, 4, 2, 32, 128), bf16),
            v((2, 2, 2, 3, 2, 256, 128), bf16),
            v((2, 2, 2, 2, 4, 256, 128), bf16),
            v((2, 256, 2176), f32),
            v((2, 256, 2176), f32),
            v((2, 256, 2176), bf16),
            v((2, 256, 128), f32),
            v((2, 256, 128), f32),
            v((2, 256, 128), bf16),
            v((128, 2176), f32),
            v((128, 128), f32),
            v((2, 128, 2048), bf16),
            v((2, 128, 256), bf16),
            v((2, 128, 256), bf16),
            v((2, 2, 2, 4, 256, 128), bf16),
            v((2, 2, 3, 2, 256, 128), bf16),
            v((2, 2, 4, 4, 2, 32, 128), bf16),
            v((2, 2, 3, 4, 2, 32, 128), bf16),
            v((2, 2, 4, 2, 32, 128), bf16),
            v((2, 2, 4, 2, 32, 128), bf16),
            pltpu.SemaphoreType.DMA((COPIES,)),
            pltpu.SemaphoreType.DMA((COPIES,)),
            pltpu.SemaphoreType.DMA((7,)),
        ],
        compiler_params=pltpu.CompilerParams(
            collective_id=0, has_side_effects=True, vmem_limit_bytes=56 * 1024 * 1024
        ),
        cost_estimate=pl.CostEstimate(flops=10**10, bytes_accessed=10**7, transcendentals=10**7),
    )(bq[0], bk[0], bv[0], pk, pv, go[0], length, prefix, count)
    return outs[0][None], outs[1][None], outs[2][None], outs[3]


def solution(mesh):
    both = ("grp", "seq")
    rows3, rows2, rows1 = P(both, None, None), P(both, None), P(both)
    return jax.shard_map(
        on_device,
        mesh=mesh,
        in_specs=(rows3, rows3, rows3, rows2, rows2, rows3, rows1, rows1, rows1),
        out_specs=(rows3, rows3, rows3, rows2),
        check_vma=False,
    )
```

```python
import functools
import math

import jax
import jax.numpy as jnp
from jax import lax
from jax.experimental import pallas as pl
from jax.experimental.pallas import tpu as pltpu
from jax.sharding import PartitionSpec as P

f32, bf16 = jnp.float32, jnp.bfloat16
MESH = pl.DeviceIdType.MESH
SCALE = 1.0 / math.sqrt(128.0)
EXP2_SCALE = math.log2(math.e) / math.sqrt(128.0)
NEG = -1e30
HALVES = (("y", "z"), ("z", "y"))
HEADS, BRANCHES, KV = 2, 2, 2


def dot(a, b, ca, cb):
    return lax.dot_general(a, b, (((ca,), (cb,)), ((), ())), preferred_element_type=f32)


def place():
    g, s = lax.axis_index("grp"), lax.axis_index("seq")
    return dict(x=((s // 4) % 2) * 2 + g // 2, y=s % 4, z=s // 8, core=g % 2)


def device(at):
    return ((at["x"] % 2) * 2 + at["core"], at["z"] * 8 + (at["x"] // 2) * 4 + at["y"])


def peer(at, axis, distance, other_core=0):
    to = dict(at)
    if axis is not None:
        to[axis] = (at[axis] + distance) % 4
    if other_core:
        to["core"] = 1 - at["core"]
    return device(to)


def kernel(
    q_hbm, bk_hbm, bv_hbm, pk_hbm, pv_hbm, go_hbm, len_ref, pfx_ref, cnt_ref,
    dq_hbm, dbk_hbm, dbv_hbm, dpk_ref,
    bk_ref, bv_ref, pk_ref, pv_ref, go_s, qb, wb, w_send, kbr, vbr, id_own, id_in, id_s,
    pack, g1, pick, ksel, s_s, p_s, ds_s, top_s, inv_s, pb_s, dk_s, dv_s, dq_s, dbk_s, dbv_s,
    dkb, r1, part_s, s2, r2, s3, r3,
    send_sem, recv_sem, local_sem,
):
    at = place()
    core = at["core"]
    other = 1 - core
    counter = [0]
    started = []

    def send(src, dst, to):
        k = counter[0]
        counter[0] += 1
        copy = pltpu.make_async_remote_copy(
            src_ref=src, dst_ref=dst, send_sem=send_sem.at[k], recv_sem=recv_sem.at[k],
            device_id=to, device_id_type=MESH,
        )
        copy.start()
        started.append(copy)
        return copy

    def cols(start, size):
        return pl.ds(pl.multiple_of(start, 128), size)

    barrier = pltpu.get_barrier_semaphore()
    partners = [peer(at, None, 0, 1)]
    partners += [peer(at, a, d, o) for a in "xyz" for d in (1, 2, 3) for o in (0, 1)]
    for to in partners:
        pl.semaphore_signal(barrier, inc=1, device_id=to, device_id_type=MESH)

    loads = [
        pltpu.make_async_copy(src, dst, local_sem.at[7 + n])
        for n, (src, dst) in enumerate(
            (
                (pk_hbm, pk_ref),
                (pv_hbm, pv_ref),
                (bk_hbm, bk_ref),
                (bv_hbm, bv_ref),
                (go_hbm, go_s),
                (q_hbm.at[:, cols(core * 2048, 2048)], qb.at[0]),
            )
        )
    ]
    for copy in loads:
        copy.start()
    id_tile = jnp.full((8, 128), pfx_ref[0], jnp.int32)
    id_own[...] = id_tile
    id_in[core] = id_tile
    loads[0].wait()
    loads[1].wait()
    for half in range(2):
        for head in range(4):
            rows, c128 = slice(half * 32, half * 32 + 32), slice(head * 128, head * 128 + 128)
            pack[half, head, 0] = pk_ref[rows, c128]
            pack[half, head, 1] = pv_ref[rows, c128]
    pl.semaphore_wait(barrier, len(partners))

    def grid(h, first):
        return (at[first], at["x"]) if h == 0 else (at["x"], at[first])

    first_copies = {}
    for h in range(HEADS):
        for half, (first, _) in enumerate(HALVES):
            here = (half, h, slice(None)) + grid(h, first) + (core,)
            first_copies[h, half] = []
            for d in range(4):
                for o in (0, 1):
                    if d == 0 and o == 0:
                        continue
                    to_core = other if o else core
                    axis = ("x" if h == 0 else first) if d else None
                    first_copies[h, half].append(
                        send(pack.at[half, 2 * to_core + h], g1.at[here], peer(at, axis, d, o))
                    )
            g1[here] = pack[half, 2 * core + h]

    def id_slot(half, d, c):
        return c if d == 0 else 2 + half * 6 + (d - 1) * 2 + c

    id_copies = [send(id_own, id_in.at[core], peer(at, None, 0, 1))]
    for half, (_, last) in enumerate(HALVES):
        for d in (1, 2, 3):
            for o in (0, 1):
                id_copies.append(send(id_own, id_in.at[id_slot(half, d, core)], peer(at, last, 4 - d, o)))

    pair = peer(at, None, 0, 1)
    loads[2].wait()
    loads[3].wait()
    pair_copies = [
        send(q_hbm.at[:, cols(other * 2048, 2048)], qb.at[1], pair),
        send(bk_ref.at[:, cols(other * 256, 256)], kbr.at[1], pair),
        send(bv_ref.at[:, cols(other * 256, 256)], vbr.at[1], pair),
    ]
    kbr[0] = bk_ref[:, cols(core * 256, 256)]
    vbr[0] = bv_ref[:, cols(core * 256, 256)]
    loads[4].wait()
    weight = lax.rsqrt(jnp.full((128, 128), cnt_ref[0], jnp.int32).astype(f32))
    live = lax.broadcasted_iota(jnp.int32, (128, 128), 0) < len_ref[0]
    weight = jnp.where(live, weight, 0.0)

    def weigh(i, _):
        theirs = go_s[:, cols(other * 2048 + i * 128, 128)].astype(f32) * weight
        w_send[:, cols(i * 128, 128)] = theirs.astype(bf16)
        ours = go_s[:, cols(core * 2048 + i * 128, 128)].astype(f32) * weight
        wb[0, :, cols(i * 128, 128)] = ours.astype(bf16)
        return 0

    lax.fori_loop(0, 16, weigh, 0)
    pair_copies.append(send(w_send, wb.at[1], pair))

    second_copies = {}
    for h in range(HEADS):
        for half in range(2):
            for copy in first_copies[h, half]:
                copy.wait_recv()
        for kv in range(KV):
            for half, (first, _) in enumerate(HALVES):
                axis = first if h == 0 else "x"
                block = g1.at[half, h, kv, at[axis]]
                second_copies[h, kv, half] = [send(block, block, peer(at, axis, d)) for d in (1, 2, 3)]

    for copy in id_copies:
        copy.wait_recv()
    id_copy = pltpu.make_async_copy(id_in.at[:, pl.ds(0, 1)], id_s, local_sem.at[2])
    id_copy.start()
    id_copy.wait()

    def prefix_of(half, d, b):
        return id_s[id_slot(half, d, other if b else core), 0, 0]

    last_copies = {}

    def last_step(h, kv, half, b):
        last = HALVES[half][1]
        for d in (1, 2, 3, 0):
            p = prefix_of(half, d, b)
            for xh in range(2):
                of = []
                for k in range(4):
                    x = xh * 2 + k // 2
                    rows = g1[half, h, kv, :, x, k % 2] if h == 0 else g1[half, h, kv, x, :, k % 2]
                    of.append(rows.reshape(128, 128))
                low = jnp.where(p == 0, of[0], of[1])
                rows = jnp.where(p < 2, low, jnp.where(p == 2, of[2], of[3]))
                if d:
                    pick[half, h, kv, d - 1, b, xh * 128:xh * 128 + 128] = rows
                else:
                    ksel[h, kv, b, half, 0, xh * 128:xh * 128 + 128] = rows
            if d:
                last_copies[h, kv, b, half, d] = send(
                    pick.at[half, h, kv, d - 1, b], ksel.at[h, kv, b, half, d], peer(at, last, d)
                )

    for h in range(HEADS):
        for b in (1, 0):
            for kv in range(KV):
                for half in range(2):
                    if b == 1:
                        for copy in second_copies[h, kv, half]:
                            copy.wait_recv()
                    last_step(h, kv, half, b)

    loads[5].wait()
    for copy in pair_copies:
        copy.wait_recv()

    spans = [(i, i * 256, 128 if i == 8 else 256) for i in (8, 0, 4, 1, 5, 2, 6, 3, 7)]

    def keys(kv, h, b, i):
        if i == 8:
            return (kbr, vbr)[kv][b, :, h * 128:h * 128 + 128]
        return ksel[h, kv, b, i // 4, i % 4]

    def rows_of(ref, t):
        h, b, j = t
        c = h * 1024 + j * 256
        return jnp.concatenate([ref[b, :, c:c + 128], ref[b, :, c + 128:c + 256]], 0)

    def split_query(t):
        query = rows_of(qb, t).astype(f32) * EXP2_SCALE
        high = query.astype(bf16)
        return jnp.concatenate([high, (query - high.astype(f32)).astype(bf16)], 1)

    def scores(t, slot, i, o, n, query, weighted):
        h, b, j = t
        if j == 0 and i < 8 and i % 4:
            last_copies[h, 0, b, i // 4, i % 4].wait_recv()
            last_copies[h, 1, b, i // 4, i % 4].wait_recv()
        k = keys(0, h, b, i)
        s = dot(query, jnp.concatenate([k, k], 1), 1, 1)
        if i == 8:
            row = lax.broadcasted_iota(jnp.int32, (256, 128), 0) % 128
            s = jnp.where(lax.broadcasted_iota(jnp.int32, (256, 128), 1) <= row, s, NEG)
        s_s[slot, :, o:o + n] = s
        top = s[:, :128] if n == 128 else jnp.maximum(s[:, :128], s[:, 128:])
        top_s[slot] = top if i == 8 else jnp.maximum(top_s[slot], top)
        p_s[slot, :, o:o + n] = dot(weighted, keys(1, h, b, i), 1, 1)

    def ds_slot(now):
        return now % 2 if now < 12 else now - 10

    def softmax(slot, keep, g):
        rows = slice(g * 32, g * 32 + 32)
        top = jnp.broadcast_to(jnp.max(top_s[slot, rows], axis=1, keepdims=True), (32, 128))
        total = mixed = None
        for o in range(0, 2176, 128):
            e = jnp.exp2(s_s[slot, rows, o:o + 128] - top)
            s_s[slot, rows, o:o + 128] = e
            ed = e * p_s[slot, rows, o:o + 128]
            total = e if total is None else total + e
            mixed = ed if mixed is None else mixed + ed
        inverse = 1.0 / jnp.sum(total, axis=1, keepdims=True)
        delta = jnp.broadcast_to(jnp.sum(mixed, axis=1, keepdims=True) * inverse, (32, 128))
        inv_s[keep, rows] = jnp.broadcast_to(inverse, (32, 128))
        for o in range(0, 2176, 128):
            e = s_s[slot, rows, o:o + 128]
            ds_s[keep, rows, o:o + 128] = (e * (p_s[slot, rows, o:o + 128] - delta)).astype(bf16)
            if o == 2048:
                pb_s[slot, rows] = (e * inverse).astype(bf16)

    def grad_query(t, keep):
        h, b, j = t
        dq = dot(ds_s[keep, :, :2048], ksel[h, 0, b].reshape(2048, 128), 1, 0)
        dq = dq + dot(ds_s[keep, :, 2048:], keys(0, h, b, 8), 1, 0)
        dq = (dq * (inv_s[keep] * SCALE)).astype(bf16)
        c = h * 1024 + j * 256
        dq_s[b, :, c:c + 128] = dq[:128]
        dq_s[b, :, c + 128:c + 256] = dq[128:]

    def local_values(t, slot, keep):
        dv = dot(pb_s[slot], rows_of(wb, t), 0, 0)
        dv_s[...] = dv if t[2] == 0 else dv_s[...] + dv
        return (rows_of(qb, t).astype(f32) * (inv_s[keep] * SCALE)).astype(bf16)

    def key_terms(t, slot, o, n, query):
        dk = dot(query, ds_s[slot, :, o:o + n], 0, 0)
        dk_s[:, o:o + n] = dk if t[2] == 0 else dk_s[:, o:o + n] + dk

    def finish_unit(h, b):
        local = slice(h * 128, h * 128 + 128)
        dbk_s[b, :, local] = dk_s[:, 2048:].T.astype(bf16)
        dbv_s[b, :, local] = dv_s[...].astype(bf16)
        for i in range(16):
            rows = slice(i % 2 * 128, i % 2 * 128 + 128)
            dkb[h, b, i // 8, i // 2 % 4, rows] = dk_s[:, i * 128:i * 128 + 128].T.astype(bf16)

    steps = [(h, b, j) for h in range(HEADS) for b in (1, 0) for j in range(4)]

    def pipeline(now):
        slot, before = now % 2, (now + 1) % 2
        ahead = steps[now] if now < 16 else None
        middle = steps[now - 1] if 0 < now <= 16 else None
        behind = steps[now - 2] if now >= 2 else None
        if ahead:
            query, weighted = split_query(ahead), rows_of(wb, ahead)
        if behind:
            keep = ds_slot(now - 2)
            scaled = local_values(behind, slot, keep)
            if now - 2 < 12:
                grad_query(behind, keep)
        for x, (i, o, n) in enumerate(spans):
            if ahead:
                scores(ahead, slot, i, o, n, query, weighted)
            if middle and x < 8:
                softmax(before, ds_slot(now - 1), x)
            if behind:
                key_terms(behind, keep, o, n, scaled)
        if behind and behind[2] == 3:
            finish_unit(behind[0], behind[1])

    def sum_last_send(h, b):
        copies = []
        for half, (_, last) in enumerate(HALVES):
            for d in (1, 2, 3):
                copies.append(
                    send(
                        dkb.at[h, b, half, d],
                        r1.at[h, half, d - 1, b],
                        peer(at, last, 4 - d),
                    )
                )
        return copies

    def sum_last(h, copies, terms, more, done):
        for copy in copies:
            copy.wait_recv()
        for half in range(2):
            ids = {(d, b): prefix_of(half, d, b) for d, b in terms}

            def block(i, _):
                rows = pl.ds(pl.multiple_of(i * 32, 32), 32)
                sums = [part_s[half, i, p] if more else jnp.zeros((32, 128), f32) for p in range(4)]
                for d, b in terms:
                    term = r1[h, half, d - 1, b, rows, :] if d else dkb[h, b, half, 0, rows, :]
                    term = term.astype(f32)
                    for p in range(4):
                        sums[p] = sums[p] + jnp.where(ids[d, b] == p, term, 0.0)
                for p in range(4):
                    if done:
                        s2[h, half, i % 4, (i // 4) * 2 + p // 2, p % 2] = sums[p].astype(bf16)
                    else:
                        part_s[half, i, p] = sums[p]
                return 0

            lax.fori_loop(0, 8, block, 0)

    early = [(d, 1) for d in range(4)] + [(0, 0)]
    late = [(d, 0) for d in (1, 2, 3)]

    def sum_first_send(h):
        return [
            send(s2.at[h, half, (at[first] + d) % 4], r2.at[h, half, d - 1], peer(at, first, d))
            for half, (first, _) in enumerate(HALVES)
            for d in (1, 2, 3)
        ]

    def sum_first(h, copies):
        for copy in copies:
            copy.wait_recv()
        for half, (first, _) in enumerate(HALVES):
            for x in range(4):
                total = s2[h, half, at[first], x].astype(f32)
                for d in range(3):
                    total = total + r2[h, half, d, x].astype(f32)
                s3[h, half, x] = total.astype(bf16)

    def sum_x_send(h):
        copies = []
        for half in range(2):
            for d in range(4):
                for o in (0, 1):
                    if d == 0 and o == 0:
                        continue
                    to_core = other if o else core
                    copies.append(
                        send(
                            s3.at[h, half, (at["x"] + d) % 4, to_core],
                            r3.at[h, half, d, o],
                            peer(at, "x" if d else None, d, o),
                        )
                    )
        return copies

    def sum_x(h, copies):
        for copy in copies:
            copy.wait_recv()
        for half in range(2):
            for o in (0, 1):
                total = (r3[h, half, 0, 1] if o else s3[h, half, at["x"], core]).astype(f32)
                for d in (1, 2, 3):
                    total = total + r3[h, half, d, o].astype(f32)
                head = 2 * (other if o else core) + h
                dpk_ref[half * 32:half * 32 + 32, cols(head * 128, 128)] = total.astype(bf16)

    local_copies = []

    def give_back(h, b, n):
        heads = cols(core * 2048 + h * 1024, 1024)
        src, dst = dq_s.at[b, :, h * 1024:h * 1024 + 1024], dq_hbm.at[:, heads]
        if b:
            return [send(src, dst, pair)]
        copy = pltpu.make_async_copy(src, dst, local_sem.at[n])
        copy.start()
        local_copies.append(copy)
        return []

    returned = []
    last_sums = {}
    mine = cols(core * 256, 256)
    for now in range(18):
        pipeline(now)
        if now in (5, 9, 13, 17):
            h, b, _ = steps[now - 2]
            last_sums[h, b] = sum_last_send(h, b)
            if now < 17:
                returned += give_back(h, b, 3 + h)
        if now == 13:
            returned.append(send(dbk_s.at[1], dbk_hbm.at[:, mine], pair))
            returned.append(send(dbv_s.at[1], dbv_hbm.at[:, mine], pair))
        if now == 14:
            sum_last(0, last_sums[0, 1] + last_sums[0, 0], early + late, False, True)
            first0 = sum_first_send(0)
    for n, (src, dst) in enumerate(((dbk_s, dbk_hbm), (dbv_s, dbv_hbm))):
        copy = pltpu.make_async_copy(src.at[0], dst.at[:, mine], local_sem.at[5 + n])
        copy.start()
        local_copies.append(copy)
    sum_last(1, last_sums[1, 1], early, False, False)
    for now in range(12, 16):
        grad_query(steps[now], ds_slot(now))
    give_back(1, 0, 4)
    sum_first(0, first0)
    x0 = sum_x_send(0)
    sum_last(1, last_sums[1, 0], late, True, True)
    first1 = sum_first_send(1)
    sum_x(0, x0)
    sum_first(1, first1)
    x1 = sum_x_send(1)
    sum_x(1, x1)

    for copy in returned:
        copy.wait_recv()
    for copy in local_copies:
        copy.wait()
    for copy in started:
        copy.wait_send()


COPIES = 13 + 28 + 4 + 24 + 48 + 24 + 12 + 28 + 4
ANY = pl.BlockSpec(memory_space=pl.ANY)
VMEM = pl.BlockSpec(memory_space=pltpu.VMEM)
SMEM = pl.BlockSpec(memory_space=pltpu.SMEM)


def place_results(dq, dbk, dbv, dpk, dq_out, dbk_out, dbv_out, dpk_out, dq_s, dbk_s, dbv_s, dpk_s, sem):
    parts = [(dq.at[pl.ds(i * 32, 32)], dq_s.at[pl.ds(i * 32, 32)], dq_out.at[pl.ds(i * 32, 32)]) for i in range(4)]
    parts += [(dbk, dbk_s, dbk_out), (dbv, dbv_s, dbv_out), (dpk, dpk_s, dpk_out)]
    reads = [pltpu.make_async_copy(a, b, sem.at[0, n]) for n, (a, b, _) in enumerate(parts)]
    writes = [pltpu.make_async_copy(b, c, sem.at[1, n]) for n, (_, b, c) in enumerate(parts)]
    for copy in reads:
        copy.start()
    for read, write in zip(reads, writes):
        read.wait()
        write.start()
    for copy in writes:
        copy.wait()


def on_device(bq, bk, bv, pk, pv, go, length, prefix, count):
    v = pltpu.VMEM
    outs = pl.pallas_call(
        kernel,
        out_shape=(
            jax.ShapeDtypeStruct((128, 4096), bf16),
            jax.ShapeDtypeStruct((128, 512), bf16),
            jax.ShapeDtypeStruct((128, 512), bf16),
            jax.ShapeDtypeStruct((64, 512), bf16),
        ),
        in_specs=[ANY] * 6 + [SMEM] * 3,
        out_specs=(ANY, ANY, ANY, VMEM),
        scratch_shapes=[
            v((128, 512), bf16),
            v((128, 512), bf16),
            v((64, 512), bf16),
            v((64, 512), bf16),
            v((128, 4096), bf16),
            v((2, 128, 2048), bf16),
            v((2, 128, 2048), bf16),
            v((128, 2048), bf16),
            v((2, 128, 256), bf16),
            v((2, 128, 256), bf16),
            v((8, 128), jnp.int32),
            v((14, 8, 128), jnp.int32),
            pltpu.SMEM((14, 1, 128), jnp.int32),
            v((2, 4, 2, 32, 128), bf16),
            v((2, 2, 2, 4, 4, 2, 32, 128), bf16),
            v((2, 2, 2, 3, 2, 256, 128), bf16),
            v((2, 2, 2, 2, 4, 256, 128), bf16),
            v((2, 256, 2176), f32),
            v((2, 256, 2176), f32),
            v((6, 256, 2176), bf16),
            v((2, 256, 128), f32),
            v((6, 256, 128), f32),
            v((2, 256, 128), bf16),
            v((128, 2176), f32),
            v((128, 128), f32),
            v((2, 128, 2048), bf16),
            v((2, 128, 256), bf16),
            v((2, 128, 256), bf16),
            v((2, 2, 2, 4, 256, 128), bf16),
            v((2, 2, 3, 2, 256, 128), bf16),
            v((2, 8, 4, 32, 128), f32),
            v((2, 2, 4, 4, 2, 32, 128), bf16),
            v((2, 2, 3, 4, 2, 32, 128), bf16),
            v((2, 2, 4, 2, 32, 128), bf16),
            v((2, 2, 4, 2, 32, 128), bf16),
            pltpu.SemaphoreType.DMA((COPIES,)),
            pltpu.SemaphoreType.DMA((COPIES,)),
            pltpu.SemaphoreType.DMA((13,)),
        ],
        compiler_params=pltpu.CompilerParams(
            collective_id=0, has_side_effects=True, vmem_limit_bytes=56 * 1024 * 1024
        ),
        cost_estimate=pl.CostEstimate(flops=10**10, bytes_accessed=10**7, transcendentals=10**7),
    )(bq[0], bk[0], bv[0], pk, pv, go[0], length, prefix, count)
    outs = pl.pallas_call(
        place_results,
        out_shape=tuple(jax.ShapeDtypeStruct(o.shape, o.dtype) for o in outs),
        in_specs=[ANY] * 4,
        out_specs=(ANY,) * 4,
        scratch_shapes=[v(o.shape, o.dtype) for o in outs] + [pltpu.SemaphoreType.DMA((2, 7))],
    )(*outs)
    return outs[0][None], outs[1][None], outs[2][None], outs[3]


def solution(mesh):
    both = ("grp", "seq")
    rows3, rows2, rows1 = P(both, None, None), P(both, None), P(both)
    return jax.shard_map(
        on_device,
        mesh=mesh,
        in_specs=(rows3, rows3, rows3, rows2, rows2, rows3, rows1, rows1, rows1),
        out_specs=(rows3, rows3, rows3, rows2),
        check_vma=False,
    )
```

```python
import functools
import math

import jax
import jax.numpy as jnp
from jax import lax
from jax.experimental import pallas as pl
from jax.experimental.pallas import tpu as pltpu
from jax.sharding import PartitionSpec as P

f32, bf16 = jnp.float32, jnp.bfloat16
MESH = pl.DeviceIdType.MESH
SCALE = 1.0 / math.sqrt(128.0)
EXP2_SCALE = math.log2(math.e) / math.sqrt(128.0)
NEG = -1e30
HALVES = (("y", "z"), ("z", "y"))
HEADS, BRANCHES, KV = 2, 2, 2


def dot(a, b, ca, cb):
    return lax.dot_general(a, b, (((ca,), (cb,)), ((), ())), preferred_element_type=f32)


def place():
    g, s = lax.axis_index("grp"), lax.axis_index("seq")
    return dict(x=((s // 4) % 2) * 2 + g // 2, y=s % 4, z=s // 8, core=g % 2)


def device(at):
    return ((at["x"] % 2) * 2 + at["core"], at["z"] * 8 + (at["x"] // 2) * 4 + at["y"])


def peer(at, axis, distance, other_core=0):
    to = dict(at)
    if axis is not None:
        to[axis] = (at[axis] + distance) % 4
    if other_core:
        to["core"] = 1 - at["core"]
    return device(to)


def kernel(
    q_hbm, bk_hbm, bv_hbm, pk_hbm, pv_hbm, go_hbm, len_ref, pfx_ref, cnt_ref,
    dq_hbm, dbk_hbm, dbv_hbm, dpk_ref,
    bk_ref, bv_ref, pk_ref, pv_ref, go_s, qb, wb, w_send, kbr, vbr, id_own, id_in, id_s,
    pack, g1, pick, ksel, s_s, p_s, ds_s, top_s, inv_s, pb_s, dk_s, dv_s, dq_s, dbk_s, dbv_s,
    dkb, r1, part_s, s2, r2, s3, r3,
    send_sem, recv_sem, local_sem,
):
    at = place()
    core = at["core"]
    other = 1 - core
    counter = [0]
    started = []

    def send(src, dst, to):
        k = counter[0]
        counter[0] += 1
        copy = pltpu.make_async_remote_copy(
            src_ref=src, dst_ref=dst, send_sem=send_sem.at[k], recv_sem=recv_sem.at[k],
            device_id=to, device_id_type=MESH,
        )
        copy.start()
        started.append(copy)
        return copy

    def cols(start, size):
        return pl.ds(pl.multiple_of(start, 128), size)

    barrier = pltpu.get_barrier_semaphore()
    partners = [peer(at, None, 0, 1)]
    partners += [peer(at, a, d, o) for a in "xyz" for d in (1, 2, 3) for o in (0, 1)]
    for to in partners:
        pl.semaphore_signal(barrier, inc=1, device_id=to, device_id_type=MESH)

    loads = [
        pltpu.make_async_copy(src, dst, local_sem.at[7 + n])
        for n, (src, dst) in enumerate(
            (
                (pk_hbm, pk_ref),
                (pv_hbm, pv_ref),
                (bk_hbm, bk_ref),
                (bv_hbm, bv_ref),
                (go_hbm, go_s),
                (q_hbm.at[:, cols(core * 2048, 2048)], qb.at[0]),
            )
        )
    ]
    for copy in loads:
        copy.start()
    id_tile = jnp.full((8, 128), pfx_ref[0], jnp.int32)
    id_own[...] = id_tile
    id_in[core] = id_tile
    loads[0].wait()
    loads[1].wait()
    for half in range(2):
        for head in range(4):
            rows, c128 = slice(half * 32, half * 32 + 32), slice(head * 128, head * 128 + 128)
            pack[half, head, 0] = pk_ref[rows, c128]
            pack[half, head, 1] = pv_ref[rows, c128]
    pl.semaphore_wait(barrier, len(partners))

    def grid(h, first):
        return (at[first], at["x"]) if h == 0 else (at["x"], at[first])

    first_copies = {}
    for h in range(HEADS):
        for half, (first, _) in enumerate(HALVES):
            here = (half, h, slice(None)) + grid(h, first) + (core,)
            first_copies[h, half] = []
            for d in range(4):
                for o in (0, 1):
                    if d == 0 and o == 0:
                        continue
                    to_core = other if o else core
                    axis = ("x" if h == 0 else first) if d else None
                    first_copies[h, half].append(
                        send(pack.at[half, 2 * to_core + h], g1.at[here], peer(at, axis, d, o))
                    )
            g1[here] = pack[half, 2 * core + h]

    def id_slot(half, d, c):
        return c if d == 0 else 2 + half * 6 + (d - 1) * 2 + c

    id_copies = [send(id_own, id_in.at[core], peer(at, None, 0, 1))]
    for half, (_, last) in enumerate(HALVES):
        for d in (1, 2, 3):
            for o in (0, 1):
                id_copies.append(send(id_own, id_in.at[id_slot(half, d, core)], peer(at, last, 4 - d, o)))

    pair = peer(at, None, 0, 1)
    loads[2].wait()
    loads[3].wait()
    pair_copies = [
        send(q_hbm.at[:, cols(other * 2048, 2048)], qb.at[1], pair),
        send(bk_ref.at[:, cols(other * 256, 256)], kbr.at[1], pair),
        send(bv_ref.at[:, cols(other * 256, 256)], vbr.at[1], pair),
    ]
    kbr[0] = bk_ref[:, cols(core * 256, 256)]
    vbr[0] = bv_ref[:, cols(core * 256, 256)]
    second_copies = {}
    for h in range(HEADS):
        for half in range(2):
            for copy in first_copies[h, half]:
                copy.wait_recv()
        for kv in range(KV):
            for half, (first, _) in enumerate(HALVES):
                axis = first if h == 0 else "x"
                block = g1.at[half, h, kv, at[axis]]
                second_copies[h, kv, half] = [send(block, block, peer(at, axis, d)) for d in (1, 2, 3)]

    loads[4].wait()
    weight = lax.rsqrt(jnp.full((128, 128), cnt_ref[0], jnp.int32).astype(f32))
    live = lax.broadcasted_iota(jnp.int32, (128, 128), 0) < len_ref[0]
    weight = jnp.where(live, weight, 0.0)

    def weigh(i, _):
        theirs = go_s[:, cols(other * 2048 + i * 128, 128)].astype(f32) * weight
        w_send[:, cols(i * 128, 128)] = theirs.astype(bf16)
        ours = go_s[:, cols(core * 2048 + i * 128, 128)].astype(f32) * weight
        wb[0, :, cols(i * 128, 128)] = ours.astype(bf16)
        return 0

    lax.fori_loop(0, 16, weigh, 0)
    pair_copies.append(send(w_send, wb.at[1], pair))

    for copy in id_copies:
        copy.wait_recv()
    id_copy = pltpu.make_async_copy(id_in.at[:, pl.ds(0, 1)], id_s, local_sem.at[2])
    id_copy.start()
    id_copy.wait()

    def prefix_of(half, d, b):
        return id_s[id_slot(half, d, other if b else core), 0, 0]

    last_copies = {}

    def last_step(h, kv, half, b):
        last = HALVES[half][1]
        for d in (1, 2, 3, 0):
            p = prefix_of(half, d, b)
            for xh in range(2):
                of = []
                for k in range(4):
                    x = xh * 2 + k // 2
                    rows = g1[half, h, kv, :, x, k % 2] if h == 0 else g1[half, h, kv, x, :, k % 2]
                    of.append(rows.reshape(128, 128))
                low = jnp.where(p == 0, of[0], of[1])
                rows = jnp.where(p < 2, low, jnp.where(p == 2, of[2], of[3]))
                if d:
                    pick[half, h, kv, d - 1, b, xh * 128:xh * 128 + 128] = rows
                else:
                    ksel[h, kv, b, half, 0, xh * 128:xh * 128 + 128] = rows
            if d:
                last_copies[h, kv, b, half, d] = send(
                    pick.at[half, h, kv, d - 1, b], ksel.at[h, kv, b, half, d], peer(at, last, d)
                )

    for h in range(HEADS):
        for b in (1, 0):
            for kv in range(KV):
                for half in range(2):
                    if b == 1:
                        for copy in second_copies[h, kv, half]:
                            copy.wait_recv()
                    last_step(h, kv, half, b)

    loads[5].wait()
    for copy in pair_copies:
        copy.wait_recv()

    spans = [(i, i * 256, 128 if i == 8 else 256) for i in (8, 0, 4, 1, 5, 2, 6, 3, 7)]

    def keys(kv, h, b, i):
        if i == 8:
            return (kbr, vbr)[kv][b, :, h * 128:h * 128 + 128]
        return ksel[h, kv, b, i // 4, i % 4]

    def rows_of(ref, t):
        h, b, j = t
        c = h * 1024 + j * 256
        return jnp.concatenate([ref[b, :, c:c + 128], ref[b, :, c + 128:c + 256]], 0)

    def split_query(t):
        query = rows_of(qb, t).astype(f32) * EXP2_SCALE
        high = query.astype(bf16)
        return jnp.concatenate([high, (query - high.astype(f32)).astype(bf16)], 1)

    def scores(t, slot, i, o, n, query, weighted):
        h, b, j = t
        if j == 0 and i < 8 and i % 4:
            last_copies[h, 0, b, i // 4, i % 4].wait_recv()
            last_copies[h, 1, b, i // 4, i % 4].wait_recv()
        k = keys(0, h, b, i)
        s = dot(query, jnp.concatenate([k, k], 1), 1, 1)
        if i == 8:
            row = lax.broadcasted_iota(jnp.int32, (256, 128), 0) % 128
            s = jnp.where(lax.broadcasted_iota(jnp.int32, (256, 128), 1) <= row, s, NEG)
        s_s[slot, :, o:o + n] = s
        top = s[:, :128] if n == 128 else jnp.maximum(s[:, :128], s[:, 128:])
        top_s[slot] = top if i == 8 else jnp.maximum(top_s[slot], top)
        p_s[slot, :, o:o + n] = dot(weighted, keys(1, h, b, i), 1, 1)

    def ds_slot(now):
        return now % 2 if now < 12 else now - 10

    def softmax(slot, keep, g):
        rows = slice(g * 32, g * 32 + 32)
        top = jnp.broadcast_to(jnp.max(top_s[slot, rows], axis=1, keepdims=True), (32, 128))
        total = mixed = None
        for o in range(0, 2176, 128):
            e = jnp.exp2(s_s[slot, rows, o:o + 128] - top)
            s_s[slot, rows, o:o + 128] = e
            ed = e * p_s[slot, rows, o:o + 128]
            total = e if total is None else total + e
            mixed = ed if mixed is None else mixed + ed
        inverse = 1.0 / jnp.sum(total, axis=1, keepdims=True)
        delta = jnp.broadcast_to(jnp.sum(mixed, axis=1, keepdims=True) * inverse, (32, 128))
        inv_s[keep, rows] = jnp.broadcast_to(inverse, (32, 128))
        for o in range(0, 2176, 128):
            e = s_s[slot, rows, o:o + 128]
            ds_s[keep, rows, o:o + 128] = (e * (p_s[slot, rows, o:o + 128] - delta)).astype(bf16)
            if o == 2048:
                pb_s[slot, rows] = (e * inverse).astype(bf16)

    def grad_query(t, keep):
        h, b, j = t
        dq = dot(ds_s[keep, :, :2048], ksel[h, 0, b].reshape(2048, 128), 1, 0)
        dq = dq + dot(ds_s[keep, :, 2048:], keys(0, h, b, 8), 1, 0)
        dq = (dq * (inv_s[keep] * SCALE)).astype(bf16)
        c = h * 1024 + j * 256
        dq_s[b, :, c:c + 128] = dq[:128]
        dq_s[b, :, c + 128:c + 256] = dq[128:]

    def local_values(t, slot, keep):
        dv = dot(pb_s[slot], rows_of(wb, t), 0, 0)
        dv_s[...] = dv if t[2] == 0 else dv_s[...] + dv
        return (rows_of(qb, t).astype(f32) * (inv_s[keep] * SCALE)).astype(bf16)

    def key_terms(t, slot, o, n, query):
        dk = dot(query, ds_s[slot, :, o:o + n], 0, 0)
        dk_s[:, o:o + n] = dk if t[2] == 0 else dk_s[:, o:o + n] + dk

    def finish_unit(h, b):
        local = slice(h * 128, h * 128 + 128)
        dbk_s[b, :, local] = dk_s[:, 2048:].T.astype(bf16)
        dbv_s[b, :, local] = dv_s[...].astype(bf16)
        for i in range(16):
            rows = slice(i % 2 * 128, i % 2 * 128 + 128)
            dkb[h, b, i // 8, i // 2 % 4, rows] = dk_s[:, i * 128:i * 128 + 128].T.astype(bf16)

    steps = [(h, b, j) for h in range(HEADS) for b in (1, 0) for j in range(4)]

    def pipeline(now):
        slot, before = now % 2, (now + 1) % 2
        ahead = steps[now] if now < 16 else None
        middle = steps[now - 1] if 0 < now <= 16 else None
        behind = steps[now - 2] if now >= 2 else None
        if ahead:
            query, weighted = split_query(ahead), rows_of(wb, ahead)
        if behind:
            keep = ds_slot(now - 2)
            scaled = local_values(behind, slot, keep)
            if now - 2 < 12:
                grad_query(behind, keep)
        for x, (i, o, n) in enumerate(spans):
            if ahead:
                scores(ahead, slot, i, o, n, query, weighted)
            if middle and x < 8:
                softmax(before, ds_slot(now - 1), x)
            if behind:
                key_terms(behind, keep, o, n, scaled)
        if behind and behind[2] == 3:
            finish_unit(behind[0], behind[1])

    def sum_last_send(h, b):
        return [
            [
                send(dkb.at[h, b, half, d], r1.at[h, half, d - 1, b], peer(at, last, 4 - d))
                for d in (2, 1, 3)
            ]
            for half, (_, last) in enumerate(HALVES)
        ]

    def sum_last(h, half, copies, terms, more, done):
        for copy in copies:
            copy.wait_recv()
        ids = {(d, b): prefix_of(half, d, b) for d, b in terms}

        def block(i, _):
            rows = pl.ds(pl.multiple_of(i * 32, 32), 32)
            sums = [part_s[half, i, p] if more else jnp.zeros((32, 128), f32) for p in range(4)]
            for d, b in terms:
                term = r1[h, half, d - 1, b, rows, :] if d else dkb[h, b, half, 0, rows, :]
                term = term.astype(f32)
                for p in range(4):
                    sums[p] = sums[p] + jnp.where(ids[d, b] == p, term, 0.0)
            for p in range(4):
                if done:
                    s2[h, half, i % 4, (i // 4) * 2 + p // 2, p % 2] = sums[p].astype(bf16)
                else:
                    part_s[half, i, p] = sums[p]
            return 0

        lax.fori_loop(0, 8, block, 0)

    early = [(d, 1) for d in range(4)] + [(0, 0)]
    late = [(d, 0) for d in (1, 2, 3)]

    def sum_first_send(h, half):
        first = HALVES[half][0]
        return [
            send(s2.at[h, half, (at[first] + d) % 4], r2.at[h, half, d - 1], peer(at, first, d))
            for d in (2, 1, 3)
        ]

    def sum_first(h, half, copies):
        for copy in copies:
            copy.wait_recv()
        for x in range(4):
            total = s2[h, half, at[HALVES[half][0]], x].astype(f32)
            for d in range(3):
                total = total + r2[h, half, d, x].astype(f32)
            s3[h, half, x] = total.astype(bf16)

    def sum_x_send(h, half):
        copies = []
        for d in (2, 1, 3, 0):
            for o in (1, 0):
                if d == 0 and o == 0:
                    continue
                to_core = other if o else core
                copies.append(
                    send(
                        s3.at[h, half, (at["x"] + d) % 4, to_core],
                        r3.at[h, half, d, o],
                        peer(at, "x" if d else None, d, o),
                    )
                )
        return copies

    def sum_x(h, half, copies):
        for copy in copies:
            copy.wait_recv()
        for o in (0, 1):
            total = (r3[h, half, 0, 1] if o else s3[h, half, at["x"], core]).astype(f32)
            for d in (1, 2, 3):
                total = total + r3[h, half, d, o].astype(f32)
            head = 2 * (other if o else core) + h
            dpk_ref[half * 32:half * 32 + 32, cols(head * 128, 128)] = total.astype(bf16)

    local_copies = []

    def give_back(h, b, n):
        heads = cols(core * 2048 + h * 1024, 1024)
        src, dst = dq_s.at[b, :, h * 1024:h * 1024 + 1024], dq_hbm.at[:, heads]
        if b:
            return [send(src, dst, pair)]
        copy = pltpu.make_async_copy(src, dst, local_sem.at[n])
        copy.start()
        local_copies.append(copy)
        return []

    returned = []
    last_sums = {}
    mine = cols(core * 256, 256)
    for now in range(18):
        pipeline(now)
        if now in (5, 9, 13, 17):
            h, b, _ = steps[now - 2]
            last_sums[h, b] = sum_last_send(h, b)
            if now < 17:
                returned += give_back(h, b, 3 + h)
        if now == 13:
            returned.append(send(dbk_s.at[1], dbk_hbm.at[:, mine], pair))
            returned.append(send(dbv_s.at[1], dbv_hbm.at[:, mine], pair))
        if now == 14:
            first0 = []
            for half in range(2):
                sum_last(0, half, last_sums[0, 1][half] + last_sums[0, 0][half], early + late, False, True)
                first0.append(sum_first_send(0, half))
    for n, (src, dst) in enumerate(((dbk_s, dbk_hbm), (dbv_s, dbv_hbm))):
        copy = pltpu.make_async_copy(src.at[0], dst.at[:, mine], local_sem.at[5 + n])
        copy.start()
        local_copies.append(copy)
    for half in range(2):
        sum_last(1, half, last_sums[1, 1][half], early, False, False)
    for now in range(12, 16):
        grad_query(steps[now], ds_slot(now))
    give_back(1, 0, 4)
    x0, first1, x1 = [], [], []
    for half in range(2):
        sum_first(0, half, first0[half])
        x0.append(sum_x_send(0, half))
    for half in range(2):
        sum_last(1, half, last_sums[1, 0][half], late, True, True)
        first1.append(sum_first_send(1, half))
    for half in range(2):
        sum_x(0, half, x0[half])
    for half in range(2):
        sum_first(1, half, first1[half])
        x1.append(sum_x_send(1, half))
    for half in range(2):
        sum_x(1, half, x1[half])

    for copy in returned:
        copy.wait_recv()
    for copy in local_copies:
        copy.wait()
    for copy in started:
        copy.wait_send()


COPIES = 13 + 28 + 4 + 24 + 48 + 24 + 12 + 28 + 4
ANY = pl.BlockSpec(memory_space=pl.ANY)
VMEM = pl.BlockSpec(memory_space=pltpu.VMEM)
SMEM = pl.BlockSpec(memory_space=pltpu.SMEM)


def place_results(dq, dbk, dbv, dpk, dq_out, dbk_out, dbv_out, dpk_out, dq_s, dbk_s, dbv_s, dpk_s, sem):
    parts = [(dq.at[pl.ds(i * 32, 32)], dq_s.at[pl.ds(i * 32, 32)], dq_out.at[pl.ds(i * 32, 32)]) for i in range(4)]
    parts += [(dbk, dbk_s, dbk_out), (dbv, dbv_s, dbv_out), (dpk, dpk_s, dpk_out)]
    reads = [pltpu.make_async_copy(a, b, sem.at[0, n]) for n, (a, b, _) in enumerate(parts)]
    writes = [pltpu.make_async_copy(b, c, sem.at[1, n]) for n, (_, b, c) in enumerate(parts)]
    for copy in reads:
        copy.start()
    for read, write in zip(reads, writes):
        read.wait()
        write.start()
    for copy in writes:
        copy.wait()


def on_device(bq, bk, bv, pk, pv, go, length, prefix, count):
    v = pltpu.VMEM
    outs = pl.pallas_call(
        kernel,
        out_shape=(
            jax.ShapeDtypeStruct((128, 4096), bf16),
            jax.ShapeDtypeStruct((128, 512), bf16),
            jax.ShapeDtypeStruct((128, 512), bf16),
            jax.ShapeDtypeStruct((64, 512), bf16),
        ),
        in_specs=[ANY] * 6 + [SMEM] * 3,
        out_specs=(ANY, ANY, ANY, VMEM),
        scratch_shapes=[
            v((128, 512), bf16),
            v((128, 512), bf16),
            v((64, 512), bf16),
            v((64, 512), bf16),
            v((128, 4096), bf16),
            v((2, 128, 2048), bf16),
            v((2, 128, 2048), bf16),
            v((128, 2048), bf16),
            v((2, 128, 256), bf16),
            v((2, 128, 256), bf16),
            v((8, 128), jnp.int32),
            v((14, 8, 128), jnp.int32),
            pltpu.SMEM((14, 1, 128), jnp.int32),
            v((2, 4, 2, 32, 128), bf16),
            v((2, 2, 2, 4, 4, 2, 32, 128), bf16),
            v((2, 2, 2, 3, 2, 256, 128), bf16),
            v((2, 2, 2, 2, 4, 256, 128), bf16),
            v((2, 256, 2176), f32),
            v((2, 256, 2176), f32),
            v((6, 256, 2176), bf16),
            v((2, 256, 128), f32),
            v((6, 256, 128), f32),
            v((2, 256, 128), bf16),
            v((128, 2176), f32),
            v((128, 128), f32),
            v((2, 128, 2048), bf16),
            v((2, 128, 256), bf16),
            v((2, 128, 256), bf16),
            v((2, 2, 2, 4, 256, 128), bf16),
            v((2, 2, 3, 2, 256, 128), bf16),
            v((2, 8, 4, 32, 128), f32),
            v((2, 2, 4, 4, 2, 32, 128), bf16),
            v((2, 2, 3, 4, 2, 32, 128), bf16),
            v((2, 2, 4, 2, 32, 128), bf16),
            v((2, 2, 4, 2, 32, 128), bf16),
            pltpu.SemaphoreType.DMA((COPIES,)),
            pltpu.SemaphoreType.DMA((COPIES,)),
            pltpu.SemaphoreType.DMA((13,)),
        ],
        compiler_params=pltpu.CompilerParams(
            collective_id=0, has_side_effects=True, vmem_limit_bytes=56 * 1024 * 1024
        ),
        cost_estimate=pl.CostEstimate(flops=10**10, bytes_accessed=10**7, transcendentals=10**7),
    )(bq[0], bk[0], bv[0], pk, pv, go[0], length, prefix, count)
    outs = pl.pallas_call(
        place_results,
        out_shape=tuple(jax.ShapeDtypeStruct(o.shape, o.dtype) for o in outs),
        in_specs=[ANY] * 4,
        out_specs=(ANY,) * 4,
        scratch_shapes=[v(o.shape, o.dtype) for o in outs] + [pltpu.SemaphoreType.DMA((2, 7))],
    )(*outs)
    return outs[0][None], outs[1][None], outs[2][None], outs[3]


def solution(mesh):
    both = ("grp", "seq")
    rows3, rows2, rows1 = P(both, None, None), P(both, None), P(both)
    return jax.shard_map(
        on_device,
        mesh=mesh,
        in_specs=(rows3, rows3, rows3, rows2, rows2, rows3, rows1, rows1, rows1),
        out_specs=(rows3, rows3, rows3, rows2),
        check_vma=False,
    )
```
